512 devices in a mesh: dp: 16 (over y, core), ctx: 32 (over z, x).
Axes of the slice: x: 4, y: 8, z: 8, core: 2. Of those that a mesh axis runs over, the one named last changes fastest.
Arguments:
- query_rows: bfloat16 [65536, 2048], P(('dp', 'ctx')), parts along dimension 0, may hold values from -130 to 130
- key_token_rows: bfloat16 [65536, 512], P(('dp', 'ctx')), parts along dimension 0, may hold values from -4 to 4
- value_token_rows: bfloat16 [65536, 512], P(('dp', 'ctx')), parts along dimension 0, may hold values from -6 to 6
- doc_lengths: int32 [256], P('dp'), parts along dimension 0, may hold values from 1 to 1536, 4096 in all
Outputs:
- attended: bfloat16 [65536, 2048], P(('dp', 'ctx')), parts along dimension 0
The draws below stay inside these ranges and needn't reach their ends.
There are 16 independent parts, one for each index of `dp`. The reference program is written for one: setup_inputs(seed, part) draws one part's arguments, and reference() takes and returns one part's arrays. A program takes and returns all parts, laid end to end along the dimension named above; each array names one. Nothing has to cross between parts.
Inputs may be any that keep to these rules, and one draw needn't show every extreme that they name: `doc_lengths`: each sequence's lengths sum to 4096; the longest document has exactly 1536 tokens.
All inputs are finite; a program needn't handle non-finite values.
Results may differ from the reference program's by a relative error of at most 0.0044.
Values may be sent and summed in bfloat16 or wider, within the bound.
A program may use at most 128 MiB of HBM per device.

```python
import math
import jax
import jax.numpy as jnp
import numpy as np
from jax import lax

LOCAL_QUERY_HEADS = 16
LOCAL_KEY_HEADS = 4
HEAD_SIZE = 128
NDOC = 16
PACKED_TOKENS = 4096


def shared_base(key):
    return jax.random.truncated_normal(key, -4.0, 4.0, (PACKED_TOKENS, LOCAL_KEY_HEADS * HEAD_SIZE), jnp.float32)


def draw_key_token_rows(key, part):
    offset_start = shared_base(key)
    return offset_start.astype(jnp.bfloat16)


def draw_query_rows(key, part):
    key = jax.random.fold_in(key, 12)
    drawn = jax.random.truncated_normal(key, -4.0, 4.0, (PACKED_TOKENS, LOCAL_QUERY_HEADS * HEAD_SIZE), jnp.float32)
    return drawn.astype(jnp.bfloat16)


def level_of(key, dims, pieces, smallest, largest):
    def one(position, blocks):
        steps = jax.random.uniform(jax.random.fold_in(jax.random.fold_in(key, 6), position), (blocks,), jnp.float32, smallest / len(pieces), largest / len(pieces))
        return jnp.repeat(jnp.exp(steps), dims[position] // blocks).reshape((-1,) + (1,) * (len(dims) - position - 1))

    factor_of = one(*pieces[0])
    for cut in pieces[1:]:
        factor_of = factor_of * one(*cut)
    return factor_of


def profile(count, total, reach, skew):
    loads = [(1 << 20) // math.isqrt(rank ** skew) + 1 for rank in range(2, count + 1)]
    spare, given = total - reach - (count - 1), [1] * (count - 1)
    while spare > 0:
        movable = [i for i in range(count - 1) if given[i] < reach]
        mass, remaining = sum([loads[i] for i in movable]), spare
        for i in movable:
            more = min(reach - given[i], max(1, remaining * loads[i] // mass), spare)
            given[i] = given[i] + more
            spare = spare - more
    return np.array([reach] + given)


def ragged_sizes(rng, count, total, bound, lean):
    if count == 2:
        one = jax.random.randint(rng, (), max(1, total - bound), min(bound, total - 1) + 1)
        return jnp.stack([one, total - one])
    tallies = jnp.asarray(profile(count, total, bound, lean), jnp.int32)
    twos = (count - 1) // 2
    source_of, receiver = tallies[1:1 + 2 * twos:2], tallies[2:2 + 2 * twos:2]
    room = jnp.minimum(source_of - 1, bound - receiver)
    shifted = jax.random.randint(jax.random.fold_in(rng, 1), (twos,), 0, 1 << 20) % (room + 1)
    tallies = tallies.at[1:1 + 2 * twos:2].set(source_of - shifted).at[2:2 + 2 * twos:2].set(receiver + shifted)
    return tallies[jax.random.permutation(jax.random.fold_in(rng, 2), count)]


def scatter_about(rng, dims, width, most, pieces=(), held_as=jnp.bfloat16):
    loudness = level_of(rng, dims, pieces, -0.22, 0.18) if pieces else 1.0
    values = jax.random.normal(rng, dims, jnp.float32) * width * loudness
    return jnp.minimum(jnp.maximum(values, -most), most).astype(held_as)


def setup_inputs(seed: int = 0, part: int = 0) -> dict:
    key_of = jax.random.split(jax.random.key(seed), 5)
    part_splits = jax.random.split(jax.random.fold_in(key_of[4], part), 5)
    query_rows = draw_query_rows(jax.random.fold_in(jax.random.fold_in(key_of[4], part), 71), part)
    key_token_rows = draw_key_token_rows(jax.random.fold_in(jax.random.fold_in(key_of[4], part), 71), part)
    value_token_rows = scatter_about(part_splits[2], (PACKED_TOKENS, LOCAL_KEY_HEADS * HEAD_SIZE), 1.0, 6.0, ((0, 32),))
    doc_lengths = ragged_sizes(part_splits[3], NDOC, PACKED_TOKENS, 3 * PACKED_TOKENS // 8, 2).astype(jnp.int32)
    return {"query_rows": query_rows, "key_token_rows": key_token_rows, "value_token_rows": value_token_rows, "doc_lengths": doc_lengths}


def reference(query_rows, key_token_rows, value_token_rows, doc_lengths):
    queries_per_group = LOCAL_QUERY_HEADS // LOCAL_KEY_HEADS
    positions = jnp.arange(PACKED_TOKENS, dtype=jnp.int32)
    bounds = jnp.cumsum(doc_lengths).astype(jnp.int32)
    doc = lax.optimization_barrier(jnp.sum((positions[:, None] >= bounds[None, :]).astype(jnp.int32), axis=1))
    key_head_split = key_token_rows.reshape(PACKED_TOKENS, LOCAL_KEY_HEADS, HEAD_SIZE).astype(jnp.float32)
    value_head_split = value_token_rows.reshape(PACKED_TOKENS, LOCAL_KEY_HEADS, HEAD_SIZE).astype(jnp.float32)
    rows_per_block = math.gcd(PACKED_TOKENS, 512)
    score_scale = 1.0 / math.sqrt(HEAD_SIZE)

    def one_block(block_number):
        start = (block_number * rows_per_block).astype(jnp.int32)
        query_tile_rows = lax.dynamic_slice_in_dim(query_rows, start, rows_per_block, 0)
        query_tile_rows = query_tile_rows.reshape(rows_per_block, LOCAL_KEY_HEADS, queries_per_group, HEAD_SIZE).astype(jnp.float32)
        scores = jnp.einsum('qkgd,tkd->kgqt', query_tile_rows, key_head_split) * score_scale
        query_pos = start + jnp.arange(rows_per_block, dtype=jnp.int32)
        query_doc = lax.dynamic_slice_in_dim(doc, start, rows_per_block, 0)
        allowed = (positions[None, :] <= query_pos[:, None]) & (doc[None, :] == query_doc[:, None])
        scores = jnp.where(allowed[None, None], scores, -jnp.inf)
        row_max = lax.optimization_barrier(jnp.max(scores, axis=-1))
        expo = jnp.exp(scores - row_max[..., None])
        total = lax.optimization_barrier(jnp.sum(expo, axis=-1))
        weights = expo.astype(jnp.bfloat16)
        weights = lax.optimization_barrier(weights).astype(jnp.float32)
        mixed = jnp.einsum('kgqt,tkd->qkgd', weights, value_head_split)
        mixed = mixed / jnp.transpose(total, (2, 0, 1))[..., None]
        return mixed.reshape(rows_per_block, LOCAL_QUERY_HEADS * HEAD_SIZE).astype(jnp.bfloat16)
    blocks = lax.map(one_block, jnp.arange(PACKED_TOKENS // rows_per_block, dtype=jnp.int32))
    return blocks.reshape(PACKED_TOKENS, LOCAL_QUERY_HEADS * HEAD_SIZE)
```

```python
import math

import jax
import jax.numpy as jnp
from jax import lax
from jax.experimental import pallas as pl
from jax.experimental.pallas import tpu as pltpu
from jax.sharding import PartitionSpec as P

HEAD = 128
ROWS = 128
SIDE = 4
REACH = 3
LANES = 128
MESH = pl.DeviceIdType.MESH
LOWEST = -1e30
RATE = math.log2(math.e) / math.sqrt(HEAD)


def kernel(
    lengths, q_hbm, k_hbm, v_hbm, out_hbm,
    q_buf, kv, lo_ref, top, total, acc, o_stage,
    loc_sem, x_send, x_recv, q_send, q_recv, z_send, z_recv, o_send, o_recv, o_loc,
):
    me = lax.axis_index("ctx")
    count = lax.axis_size("ctx")
    z, x = me // SIDE, me % SIDE
    base = z * SIDE

    def mate(d):
        return base + (x + d) % SIDE

    above = (me + SIDE) % count
    below = (me + count - SIDE) % count

    def head_cols(ref, head, width):
        return ref.at[:, pl.ds(pl.multiple_of(head * width, width), width)]

    local = [
        pltpu.make_async_copy(head_cols(k_hbm, x, HEAD), kv.at[0, x, 0], loc_sem.at[0]),
        pltpu.make_async_copy(head_cols(v_hbm, x, HEAD), kv.at[0, x, 1], loc_sem.at[1]),
        pltpu.make_async_copy(head_cols(q_hbm, x, SIDE * HEAD), q_buf.at[x], loc_sem.at[2]),
    ]
    for copy in local:
        copy.start()

    barrier = pltpu.get_barrier_semaphore()
    for other in (mate(1), mate(2), mate(3), above, below):
        pl.semaphore_signal(barrier, inc=1, device_id={"ctx": other}, device_id_type=MESH)

    def starts(b, carry):
        pos = (base + b) * ROWS + lax.broadcasted_iota(jnp.int32, (ROWS, LANES), 0)
        lo = jnp.zeros((ROWS, LANES), jnp.int32)
        bound = jnp.int32(0)
        for i in range(lengths.shape[0]):
            bound = bound + lengths[i]
            lo = jnp.where(pos >= bound, bound, lo)
        lo_ref[b] = lo
        return carry

    lax.fori_loop(0, SIDE, starts, 0)
    pl.semaphore_wait(barrier, 5)

    def remote(src, dst, send, recv, to):
        return pltpu.make_async_remote_copy(
            src_ref=src, dst_ref=dst, send_sem=send, recv_sem=recv,
            device_id={"ctx": to}, device_id_type=MESH,
        )

    kv_x = {}
    for d in (1, 3, 2):
        to = (x + d) % SIDE
        kv_x[d] = [
            remote(head_cols(ref, to, HEAD), kv.at[0, x, j], x_send.at[d - 1, j], x_recv.at[d - 1, j], mate(d))
            for j, ref in enumerate((k_hbm, v_hbm))
        ]
        for copy in kv_x[d]:
            copy.start()

    def hop(row, piece, slot):
        return remote(kv.at[row, piece], kv.at[row + 1, piece], z_send.at[row, slot], z_recv.at[row, slot], above)

    order = [(x, 0), ((x + 3) % SIDE, 1), ((x + 1) % SIDE, 3), ((x + 2) % SIDE, 2)]
    local[0].wait()
    local[1].wait()
    hops = []
    for slot, (piece, d) in enumerate(order):
        if d:
            for copy in kv_x[d]:
                copy.wait_recv()
        copy = hop(0, piece, slot)
        copy.start()
        hops.append(copy)
        if slot == 0:
            q_x = {}
            for d2 in (1, 3, 2):
                q_x[d2] = remote(
                    head_cols(q_hbm, (x + d2) % SIDE, SIDE * HEAD), q_buf.at[x],
                    q_send.at[d2 - 1], q_recv.at[d2 - 1], mate(d2),
                )
                q_x[d2].start()
    local[2].wait()
    for d in (1, 3, 2):
        q_x[d].wait_recv()

    def attend(b, row, first_piece, pieces, first=False):
        n = pieces * ROWS
        q = q_buf[b]
        q4 = jnp.concatenate([q[:, h * HEAD:(h + 1) * HEAD] for h in range(SIDE)], axis=0)
        k = kv[row, pl.ds(first_piece, pieces), 0].reshape(n, HEAD)
        v = kv[row, pl.ds(first_piece, pieces), 1].reshape(n, HEAD)
        s4 = lax.dot_general(q4, k, (((1,), (1,)), ((), ())), preferred_element_type=jnp.float32)
        key_pos = (base - row * SIDE + first_piece) * ROWS + lax.broadcasted_iota(jnp.int32, (ROWS, n), 1)
        lo = jnp.concatenate([lo_ref[b]] * pieces, axis=1)
        allowed = key_pos >= lo
        if first:
            q_pos = (base + b) * ROWS + lax.broadcasted_iota(jnp.int32, (ROWS, n), 0)
            allowed = allowed & (key_pos <= q_pos)
        for h in range(SIDE):
            at = pl.ds(h * ROWS, ROWS)
            s = jnp.where(allowed, s4[h * ROWS:(h + 1) * ROWS], LOWEST)
            peak = jnp.broadcast_to(jnp.max(s, axis=1, keepdims=True), (ROWS, LANES))
            if not first:
                old = top[b, at]
                peak = jnp.maximum(old, peak)
                fade = jnp.exp2((old - peak) * RATE)
            expo = jnp.exp2((s - jnp.concatenate([peak] * pieces, axis=1)) * RATE)
            sums = jnp.broadcast_to(jnp.sum(expo, axis=1, keepdims=True), (ROWS, LANES))
            mixed = jnp.dot(expo.astype(jnp.bfloat16), v, preferred_element_type=jnp.float32)
            if first:
                total[b, at] = sums
                acc[b, at] = mixed
            else:
                total[b, at] = total[b, at] * fade + sums
                acc[b, at] = acc[b, at] * fade + mixed
            top[b, at] = peak

    def whole_row(row, first=False):
        def step(b, carry):
            attend(b, row, 0, SIDE, first)
            return carry

        lax.fori_loop(0, SIDE, step, 0)

    whole_row(0, True)

    for slot, (piece, d) in enumerate(order):
        hops[slot].wait_recv()
        copy = hop(1, piece, slot)
        copy.start()
        hops.append(copy)
    whole_row(1)
    for slot in range(SIDE):
        hops[SIDE + slot].wait_recv()
    last = []
    for slot, piece in enumerate((3, 2, 1, 0)):
        copy = hop(2, piece, slot)
        copy.start()
        last.append(copy)
    whole_row(2)

    outs = []
    for slot, b in enumerate((3, 2, 1, 0)):
        if b == 0:
            attend(b, 3, 1, 3)
        last[slot].wait_recv()
        if b == 0:
            attend(b, 3, 0, 1)
        else:
            attend(b, 3, b, SIDE - b)
        for h in range(SIDE):
            at = pl.ds(h * ROWS, ROWS)
            o_stage[b, :, h * HEAD:(h + 1) * HEAD] = (acc[b, at] / total[b, at]).astype(jnp.bfloat16)
        d = (b + SIDE - x) % SIDE
        home = head_cols(out_hbm, x, SIDE * HEAD)
        away = remote(o_stage.at[b], home, o_send.at[b], o_recv.at[x], base + b)
        stay = pltpu.make_async_copy(o_stage.at[b], home, o_loc)
        outs.append((b, away, stay))

        @pl.when(x == b)
        def _():
            stay.start()

        @pl.when(x != b)
        def _():
            away.start()

    for b, away, stay in outs:
        @pl.when(x == b)
        def _():
            stay.wait()

        @pl.when(x != b)
        def _():
            away.wait_send()

    for b in range(SIDE):
        @pl.when(x != b)
        def _():
            remote(
                o_stage.at[b], head_cols(out_hbm, b, SIDE * HEAD), o_send.at[b], o_recv.at[b], base + b
            ).wait_recv()

    for d in (1, 2, 3):
        for copy in kv_x[d]:
            copy.wait_send()
        q_x[d].wait_send()
    for copy in hops + last:
        copy.wait_send()


def body(q, k, v, lengths):
    any_spec = pl.BlockSpec(memory_space=pl.ANY)
    dma = pltpu.SemaphoreType.DMA
    return pl.pallas_call(
        kernel,
        out_shape=jax.ShapeDtypeStruct(q.shape, jnp.bfloat16),
        in_specs=[pl.BlockSpec(memory_space=pltpu.SMEM), any_spec, any_spec, any_spec],
        out_specs=any_spec,
        scratch_shapes=[
            pltpu.VMEM((SIDE, ROWS, SIDE * HEAD), jnp.bfloat16),
            pltpu.VMEM((REACH + 1, SIDE, 2, ROWS, HEAD), jnp.bfloat16),
            pltpu.VMEM((SIDE, ROWS, LANES), jnp.int32),
            pltpu.VMEM((SIDE, SIDE * ROWS, LANES), jnp.float32),
            pltpu.VMEM((SIDE, SIDE * ROWS, LANES), jnp.float32),
            pltpu.VMEM((SIDE, SIDE * ROWS, HEAD), jnp.float32),
            pltpu.VMEM((SIDE, ROWS, SIDE * HEAD), jnp.bfloat16),
            dma((3,)), dma((3, 2)), dma((3, 2)), dma((3,)), dma((3,)),
            dma((REACH, SIDE)), dma((REACH, SIDE)), dma((SIDE,)), dma((SIDE,)), dma(()),
        ],
        compiler_params=pltpu.CompilerParams(
            collective_id=0, has_side_effects=True, vmem_limit_bytes=40 * 1024 * 1024
        ),
        name="attention",
    )(lengths, q, k, v)


def solution(mesh):
    in_specs = (P(("dp", "ctx"), None), P(("dp", "ctx"), None), P(("dp", "ctx"), None), P("dp"))
    out_specs = P(("dp", "ctx"), None)
    return jax.shard_map(body, mesh=mesh, in_specs=in_specs, out_specs=out_specs, check_vma=False)
```

```python
import math

import jax
import jax.numpy as jnp
from jax import lax
from jax.experimental import pallas as pl
from jax.experimental.pallas import tpu as pltpu
from jax.sharding import PartitionSpec as P

HEAD = 128
ROWS = 128
SIDE = 4
REACH = 3
LANES = 128
WIDE = SIDE * HEAD
MESH = pl.DeviceIdType.MESH
LOWEST = -1e30
RATE = math.log2(math.e) / math.sqrt(HEAD)


def kernel(
    lengths_hbm, q_hbm, k_hbm, v_hbm, out_hbm,
    lengths, q_buf, kv, lo_ref, top, total, acc, o_stage,
    loc_sem, x_send, x_recv, z_send, z_recv, o_send, o_recv,
):
    me = lax.axis_index("ctx")
    count = lax.axis_size("ctx")
    depth = count // SIDE
    z, x = me // SIDE, me % SIDE
    base = z * SIDE
    left, right, far = (x + 3) % SIDE, (x + 1) % SIDE, (x + 2) % SIDE
    above = (me + SIDE) % count
    below = (me + count - SIDE) % count

    def held(row, piece):
        return (REACH - row) * SIDE + piece

    def cols(ref, head, width, start=0, rows=ROWS):
        return ref.at[pl.ds(start, rows), pl.ds(pl.multiple_of(head * width, width), width)]

    local = [
        pltpu.make_async_copy(cols(k_hbm, x, HEAD), kv.at[held(0, x), 0], loc_sem.at[0]),
        pltpu.make_async_copy(cols(v_hbm, x, HEAD), kv.at[held(0, x), 1], loc_sem.at[1]),
        pltpu.make_async_copy(lengths_hbm, lengths, loc_sem.at[2]),
        pltpu.make_async_copy(cols(q_hbm, x, WIDE), q_buf.at[x], loc_sem.at[3]),
    ]
    for copy in local:
        copy.start()

    barrier = pltpu.get_barrier_semaphore()

    def greet(other):
        pl.semaphore_signal(barrier, inc=1, device_id={"ctx": other}, device_id_type=MESH)

    for mate in (left, right, far):
        greet(base + mate)
    pl.when(z > 0)(lambda: greet(below))
    pl.when(z < depth - 1)(lambda: greet(above))

    pl.semaphore_wait(barrier, 3 + jnp.where(z > 0, 1, 0) + jnp.where(z < depth - 1, 1, 0))

    def remote(src, dst, send, recv, to):
        return pltpu.make_async_remote_copy(
            src_ref=src, dst_ref=dst, send_sem=send, recv_sem=recv,
            device_id={"ctx": to}, device_id_type=MESH,
        )

    def x_copy(slot, src, dst, to):
        return remote(src, dst, x_send.at[slot], x_recv.at[slot], base + to)

    def pair(slot, to):
        return [
            x_copy(slot, cols(k_hbm, to, HEAD), kv.at[held(0, x), 0], to),
            x_copy(slot + 1, cols(v_hbm, to, HEAD), kv.at[held(0, x), 1], to),
        ]

    kv_out = {"right": pair(0, right), "left": pair(2, left), "far": pair(4, far)}
    q_out = {
        "right": x_copy(6, cols(q_hbm, right, WIDE), q_buf.at[x], right),
        "left": x_copy(7, cols(q_hbm, left, WIDE), q_buf.at[x], left),
        "far": x_copy(8, cols(q_hbm, far, WIDE), q_buf.at[x], far),
    }
    for copy in kv_out["right"] + kv_out["left"]:
        copy.start()
    for copy in kv_out["far"]:
        copy.start()

    class Hop:
        def __init__(self, row, piece, slot):
            self.row = row
            self.copy = remote(
                kv.at[held(row, piece)], kv.at[held(row + 1, piece)], z_send.at[row, slot], z_recv.at[row, slot], above
            )
            self.sends = (z >= row) & (z < depth - 1)

        def start(self):
            pl.when(self.sends)(self.copy.start)

        def wait_send(self):
            pl.when(self.sends)(self.copy.wait_send)

        def wait_recv(self):
            pl.when(z > self.row)(self.copy.wait_recv)

    order = (
        (x, left, right, far),
        (x, left, jnp.maximum(right, far), jnp.minimum(right, far)),
        (3, 2, 1, 0),
    )
    hops = [[Hop(row, piece, slot) for slot, piece in enumerate(order[row])] for row in range(REACH)]

    local[0].wait()
    local[1].wait()
    hops[0][0].start()
    def clear(b, carry):
        top[b] = jnp.full((WIDE, LANES), LOWEST, jnp.float32)
        total[b] = jnp.zeros((WIDE, LANES), jnp.float32)
        acc[b] = jnp.zeros((WIDE, HEAD), jnp.float32)
        return carry

    lax.fori_loop(0, SIDE, clear, 0)

    def blank(i, carry):
        kv[i] = jnp.zeros((2, ROWS, HEAD), jnp.bfloat16)
        return carry

    lax.fori_loop(0, SIDE * jnp.maximum(REACH - z, 0), blank, 0)
    local[2].wait()

    def starts(b, carry):
        pos = (base + b) * ROWS + lax.broadcasted_iota(jnp.int32, (ROWS, LANES), 0)
        lo = jnp.zeros((ROWS, LANES), jnp.int32)
        bound = jnp.int32(0)
        for i in range(lengths.shape[0]):
            bound = bound + lengths[i]
            lo = jnp.where(pos >= bound, bound, lo)
        lo_ref[b] = lo
        return carry

    lax.fori_loop(0, SIDE, starts, 0)
    for copy in kv_out["right"]:
        copy.wait_recv()
    hops[0][1].start()
    for copy in kv_out["left"]:
        copy.wait_recv()
    hops[0][2].start()
    for copy in q_out.values():
        copy.start()
    for copy in kv_out["far"]:
        copy.wait_recv()
    hops[0][3].start()
    for slot in (0, 1):
        hops[0][slot].wait_recv()
        hops[1][slot].start()
    local[3].wait()

    def attend(b, first, pieces, causal=False):
        n = pieces * ROWS
        heads = [pl.ds(h * ROWS, ROWS) for h in range(SIDE)]
        q = q_buf[b]
        q4 = jnp.concatenate([q[:, h * HEAD:(h + 1) * HEAD] for h in range(SIDE)], axis=0)
        k = kv[pl.ds(first, pieces), 0].reshape(n, HEAD)
        v = kv[pl.ds(first, pieces), 1].reshape(n, HEAD)
        s4 = lax.dot_general(q4, k, (((1,), (1,)), ((), ())), preferred_element_type=jnp.float32)
        start = (base - REACH * SIDE + first) * ROWS
        key_pos = start + lax.broadcasted_iota(jnp.int32, (ROWS, n), 1)
        allowed = key_pos >= jnp.concatenate([lo_ref[b]] * pieces, axis=1)
        if causal:
            allowed = allowed & (key_pos <= (base + b) * ROWS + lax.broadcasted_iota(jnp.int32, (ROWS, n), 0))
        olds = [(top[b, at], total[b, at], acc[b, at]) for at in heads]
        news = []
        for h, (old_top, old_total, old_acc) in enumerate(olds):
            s = jnp.where(allowed, s4[h * ROWS:(h + 1) * ROWS], LOWEST)
            peak = jnp.maximum(old_top, jnp.broadcast_to(jnp.max(s, axis=1, keepdims=True), (ROWS, LANES)))
            fade = jnp.exp2((old_top - peak) * RATE)
            expo = jnp.exp2((s - jnp.concatenate([peak] * pieces, axis=1)) * RATE)
            sums = old_total * fade
            for i in range(pieces):
                sums = sums + expo[:, i * LANES:(i + 1) * LANES]
            mixed = jnp.dot(expo.astype(jnp.bfloat16), v, preferred_element_type=jnp.float32)
            news.append((peak, sums, old_acc * fade + mixed))
        for at, (peak, sums, mixed) in zip(heads, news):
            top[b, at] = peak
            total[b, at] = sums
            acc[b, at] = mixed

    def finish(b):
        for h in range(SIDE):
            at = pl.ds(h * ROWS, ROWS)
            sums = jnp.broadcast_to(jnp.sum(total[b, at], axis=1, keepdims=True), (ROWS, LANES))
            o_stage[b, :, h * HEAD:(h + 1) * HEAD] = (acc[b, at] / sums).astype(jnp.bfloat16)

    def block(step, carry):
        @pl.when(step == 0)
        def _():
            for slot in (2, 3):
                hops[0][slot].wait_recv()
            for slot in (2, 3):
                hops[1][slot].start()

        @pl.when(step == 1)
        def _():
            q_out["right"].wait_recv()

        @pl.when(step == 2)
        def _():
            q_out["left"].wait_recv()

        @pl.when(step == 3)
        def _():
            q_out["far"].wait_recv()
            for slot in (0, 1, 2):
                hops[1][slot].wait_recv()
            hops[2][0].start()

        shift = jnp.where(step == 0, 0, jnp.where(step == 1, 3, step - 1))
        attend((x + shift) % SIDE, 2 * SIDE, 2 * SIDE, True)
        return carry

    lax.fori_loop(0, SIDE, block, 0)
    hops[1][3].wait_recv()
    for slot in (1, 2, 3):
        hops[2][slot].start()

    def o_copy(kind, b, src, dst, to):
        return remote(src, dst, o_send.at[kind, b], o_recv.at[kind, b], base + to)

    def output(b, name):
        near = cols(out_hbm, x, WIDE)
        return {
            "stay": lambda: pltpu.make_async_copy(o_stage.at[b], near, loc_sem.at[0]),
            "right": lambda: o_copy(0, b, o_stage.at[b], near, right),
            "left": lambda: o_copy(1, b, o_stage.at[b], near, left),
            "far": lambda: o_copy(2, b, o_stage.at[b], near, far),
        }[name]()

    @pl.when(z >= 2)
    def _():
        def ahead(b, carry):
            attend(b, SIDE, SIDE)
            return carry

        lax.fori_loop(0, 2, ahead, 0)

    for slot, b in enumerate((3, 2, 1, 0)):
        if b == 0:
            pl.when(z >= REACH)(lambda: attend(b, 1, SIDE - 1))
        hops[2][slot].wait_recv()
        if b == 0:
            pl.when(z >= REACH)(lambda: attend(b, 0, 1))
        elif b == 1:
            pl.when(z >= REACH)(lambda: attend(b, 1, SIDE - 1))
        else:
            pl.when(z >= 2)(lambda: attend(b, b, 2 * SIDE - b))
        finish(b)
        pl.when(x == b)(lambda: output(b, "stay").start())
        pl.when(right == b)(lambda: output(b, "right").start())
        pl.when(left == b)(lambda: output(b, "left").start())
        pl.when(far == b)(lambda: output(b, "far").start())

    for name in ("right", "left", "far"):
        output(x, name).wait_recv()
    output(x, "stay").wait()
    output(right, "right").wait_send()
    output(left, "left").wait_send()
    output(far, "far").wait_send()
    for copies in (*kv_out.values(), q_out.values(), *hops):
        for copy in copies:
            copy.wait_send()


def body(q, k, v, lengths):
    far_spec = pl.BlockSpec(memory_space=pltpu.HBM)
    dma = pltpu.SemaphoreType.DMA
    q, k, v, lengths = (pltpu.with_memory_space_constraint(a, pltpu.HBM) for a in (q, k, v, lengths))
    return pl.pallas_call(
        kernel,
        out_shape=jax.ShapeDtypeStruct(q.shape, jnp.bfloat16),
        in_specs=[far_spec] * 4,
        out_specs=pl.BlockSpec(memory_space=pl.ANY),
        scratch_shapes=[
            pltpu.SMEM(lengths.shape, jnp.int32),
            pltpu.VMEM((SIDE, ROWS, WIDE), jnp.bfloat16),
            pltpu.VMEM(((REACH + 1) * SIDE, 2, ROWS, HEAD), jnp.bfloat16),
            pltpu.VMEM((SIDE, ROWS, LANES), jnp.int32),
            pltpu.VMEM((SIDE, WIDE, LANES), jnp.float32),
            pltpu.VMEM((SIDE, WIDE, LANES), jnp.float32),
            pltpu.VMEM((SIDE, WIDE, HEAD), jnp.float32),
            pltpu.VMEM((SIDE, ROWS, WIDE), jnp.bfloat16),
            dma((4,)), dma((9,)), dma((9,)), dma((REACH, SIDE)), dma((REACH, SIDE)), dma((3, SIDE)), dma((3, SIDE)),
        ],
        compiler_params=pltpu.CompilerParams(
            collective_id=0, has_side_effects=True, vmem_limit_bytes=32 * 1024 * 1024
        ),
        name="attention",
    )(lengths, q, k, v)


def solution(mesh):
    in_specs = (P(("dp", "ctx"), None), P(("dp", "ctx"), None), P(("dp", "ctx"), None), P("dp"))
    out_specs = P(("dp", "ctx"), None)
    return jax.shard_map(body, mesh=mesh, in_specs=in_specs, out_specs=out_specs, check_vma=False)
```

```python
import math

import jax
import jax.numpy as jnp
from jax import lax
from jax.experimental import pallas as pl
from jax.experimental.pallas import tpu as pltpu
from jax.sharding import PartitionSpec as P

HEAD = 128
ROWS = 128
SIDE = 4
REACH = 3
LANES = 128
WIDE = SIDE * HEAD
MESH = pl.DeviceIdType.MESH
LOWEST = -1e30
RATE = math.log2(math.e) / math.sqrt(HEAD)


def kernel(
    lengths_hbm, q_hbm, k_hbm, v_hbm, out_hbm,
    lengths, q_buf, kv, lo_ref, top, total, acc, o_stage,
    loc_sem, x_send, x_recv, z_send, z_recv, o_send, o_recv,
):
    me = lax.axis_index("ctx")
    count = lax.axis_size("ctx")
    depth = count // SIDE
    z, x = me // SIDE, me % SIDE
    base = z * SIDE
    left, right, far = (x + 3) % SIDE, (x + 1) % SIDE, (x + 2) % SIDE
    above = (me + SIDE) % count
    below = (me + count - SIDE) % count

    def held(row, piece):
        return (REACH - row) * SIDE + piece

    def cols(ref, head, width, start=0, rows=ROWS):
        return ref.at[pl.ds(start, rows), pl.ds(pl.multiple_of(head * width, width), width)]

    local = [
        pltpu.make_async_copy(cols(k_hbm, x, HEAD), kv.at[held(0, x), 0], loc_sem.at[0]),
        pltpu.make_async_copy(cols(v_hbm, x, HEAD), kv.at[held(0, x), 1], loc_sem.at[1]),
        pltpu.make_async_copy(lengths_hbm, lengths, loc_sem.at[2]),
        pltpu.make_async_copy(cols(q_hbm, x, WIDE), q_buf.at[x], loc_sem.at[3]),
    ]

    barrier = pltpu.get_barrier_semaphore()

    def greet(other):
        pl.semaphore_signal(barrier, inc=1, device_id={"ctx": other}, device_id_type=MESH)

    for mate in (left, right, far):
        greet(base + mate)
    pl.when(z > 0)(lambda: greet(below))
    pl.when(z < depth - 1)(lambda: greet(above))

    for copy in local:
        copy.start()
    pl.semaphore_wait(barrier, 3 + jnp.where(z > 0, 1, 0) + jnp.where(z < depth - 1, 1, 0))

    def remote(src, dst, send, recv, to):
        return pltpu.make_async_remote_copy(
            src_ref=src, dst_ref=dst, send_sem=send, recv_sem=recv,
            device_id={"ctx": to}, device_id_type=MESH,
        )

    def x_copy(slot, src, dst, to):
        return remote(src, dst, x_send.at[slot], x_recv.at[slot], base + to)

    def pair(slot, to):
        return [
            x_copy(slot, cols(k_hbm, to, HEAD), kv.at[held(0, x), 0], to),
            x_copy(slot + 1, cols(v_hbm, to, HEAD), kv.at[held(0, x), 1], to),
        ]

    kv_out = {"right": pair(0, right), "left": pair(2, left), "far": pair(4, far)}
    q_out = {
        "right": x_copy(6, cols(q_hbm, right, WIDE), q_buf.at[x], right),
        "left": x_copy(7, cols(q_hbm, left, WIDE), q_buf.at[x], left),
        "far": x_copy(8, cols(q_hbm, far, WIDE), q_buf.at[x], far),
    }
    for copy in kv_out["right"] + kv_out["left"]:
        copy.start()
    for copy in kv_out["far"]:
        copy.start()

    class Hop:
        def __init__(self, row, piece, slot):
            self.row = row
            self.copy = remote(
                kv.at[held(row, piece)], kv.at[held(row + 1, piece)], z_send.at[row, slot], z_recv.at[row, slot], above
            )
            self.sends = (z >= row) & (z < depth - 1)

        def start(self):
            pl.when(self.sends)(self.copy.start)

        def wait_send(self):
            pl.when(self.sends)(self.copy.wait_send)

        def wait_recv(self):
            pl.when(z > self.row)(self.copy.wait_recv)

    order = (
        (x, left, right, far),
        (x, left, jnp.maximum(right, far), jnp.minimum(right, far)),
        (3, 2, 1, 0),
    )
    hops = [[Hop(row, piece, slot) for slot, piece in enumerate(order[row])] for row in range(REACH)]

    local[0].wait()
    local[1].wait()
    hops[0][0].start()
    def clear(b, carry):
        top[b] = jnp.full((WIDE, LANES), LOWEST, jnp.float32)
        total[b] = jnp.zeros((WIDE, LANES), jnp.float32)
        acc[b] = jnp.zeros((WIDE, HEAD), jnp.float32)
        return carry

    lax.fori_loop(0, SIDE, clear, 0)

    def blank(i, carry):
        kv[i] = jnp.zeros((2, ROWS, HEAD), jnp.bfloat16)
        return carry

    lax.fori_loop(0, SIDE * jnp.maximum(REACH - z, 0), blank, 0)
    local[2].wait()

    def starts(b, carry):
        pos = (base + b) * ROWS + lax.broadcasted_iota(jnp.int32, (ROWS, LANES), 0)
        lo = jnp.zeros((ROWS, LANES), jnp.int32)
        bound = jnp.int32(0)
        for i in range(lengths.shape[0]):
            bound = bound + lengths[i]
            lo = jnp.where(pos >= bound, bound, lo)
        lo_ref[b] = lo
        return carry

    lax.fori_loop(0, SIDE, starts, 0)
    for copy in kv_out["right"]:
        copy.wait_recv()
    hops[0][1].start()
    for copy in kv_out["left"]:
        copy.wait_recv()
    hops[0][2].start()
    for copy in kv_out["far"]:
        copy.wait_recv()
    hops[0][3].start()
    for copy in q_out.values():
        copy.start()
    for slot in (0, 1):
        hops[0][slot].wait_recv()
        hops[1][slot].start()
    local[3].wait()

    def attend(b, first, pieces, causal=False):
        n = pieces * ROWS
        heads = [pl.ds(h * ROWS, ROWS) for h in range(SIDE)]
        q = q_buf[b]
        q4 = jnp.concatenate([q[:, h * HEAD:(h + 1) * HEAD] for h in range(SIDE)], axis=0)
        k = kv[pl.ds(first, pieces), 0].reshape(n, HEAD)
        v = kv[pl.ds(first, pieces), 1].reshape(n, HEAD)
        s4 = lax.dot_general(q4, k, (((1,), (1,)), ((), ())), preferred_element_type=jnp.float32)
        start = (base - REACH * SIDE + first) * ROWS
        key_pos = start + lax.broadcasted_iota(jnp.int32, (ROWS, n), 1)
        allowed = key_pos >= jnp.concatenate([lo_ref[b]] * pieces, axis=1)
        if causal:
            allowed = allowed & (key_pos <= (base + b) * ROWS + lax.broadcasted_iota(jnp.int32, (ROWS, n), 0))
        olds = [(top[b, at], total[b, at], acc[b, at]) for at in heads]
        news = []
        for h, (old_top, old_total, old_acc) in enumerate(olds):
            s = jnp.where(allowed, s4[h * ROWS:(h + 1) * ROWS], LOWEST)
            peak = jnp.maximum(old_top, jnp.broadcast_to(jnp.max(s, axis=1, keepdims=True), (ROWS, LANES)))
            fade = jnp.exp2((old_top - peak) * RATE)
            expo = jnp.exp2((s - jnp.concatenate([peak] * pieces, axis=1)) * RATE)
            sums = old_total * fade
            for i in range(pieces):
                sums = sums + expo[:, i * LANES:(i + 1) * LANES]
            mixed = jnp.dot(expo.astype(jnp.bfloat16), v, preferred_element_type=jnp.float32)
            news.append((peak, sums, old_acc * fade + mixed))
        for at, (peak, sums, mixed) in zip(heads, news):
            top[b, at] = peak
            total[b, at] = sums
            acc[b, at] = mixed

    def finish(b):
        for h in range(SIDE):
            at = pl.ds(h * ROWS, ROWS)
            sums = jnp.broadcast_to(jnp.sum(total[b, at], axis=1, keepdims=True), (ROWS, LANES))
            o_stage[b, :, h * HEAD:(h + 1) * HEAD] = (acc[b, at] / sums).astype(jnp.bfloat16)

    def block(step, carry):
        @pl.when(step == 0)
        def _():
            for slot in (2, 3):
                hops[0][slot].wait_recv()
            for slot in (2, 3):
                hops[1][slot].start()

        @pl.when(step == 1)
        def _():
            q_out["right"].wait_recv()

        @pl.when(step == 2)
        def _():
            q_out["left"].wait_recv()

        @pl.when(step == 3)
        def _():
            q_out["far"].wait_recv()
            for slot in (0, 1, 2):
                hops[1][slot].wait_recv()
            hops[2][0].start()

        shift = jnp.where(step == 0, 0, jnp.where(step == 1, 3, step - 1))
        attend((x + shift) % SIDE, 2 * SIDE, 2 * SIDE, True)
        return carry

    lax.fori_loop(0, SIDE, block, 0)
    hops[1][3].wait_recv()
    for slot in (1, 2, 3):
        hops[2][slot].start()

    def o_copy(kind, b, src, dst, to):
        return remote(src, dst, o_send.at[kind, b], o_recv.at[kind, b], base + to)

    def output(b, name):
        near = cols(out_hbm, x, WIDE)
        return {
            "stay": lambda: pltpu.make_async_copy(o_stage.at[b], near, loc_sem.at[0]),
            "right": lambda: o_copy(0, b, o_stage.at[b], near, right),
            "left": lambda: o_copy(1, b, o_stage.at[b], near, left),
            "far": lambda: o_copy(2, b, o_stage.at[b], near, far),
        }[name]()

    @pl.when(z >= 2)
    def _():
        def ahead(b, carry):
            attend(b, SIDE, SIDE)
            return carry

        lax.fori_loop(0, 2, ahead, 0)

    for slot, b in enumerate((3, 2, 1, 0)):
        if b == 0:
            pl.when(z >= REACH)(lambda: attend(b, 1, SIDE - 1))
        hops[2][slot].wait_recv()
        if b == 0:
            pl.when(z >= REACH)(lambda: attend(b, 0, 1))
        elif b == 1:
            pl.when(z >= REACH)(lambda: attend(b, 1, SIDE - 1))
        else:
            pl.when(z >= 2)(lambda: attend(b, b, 2 * SIDE - b))
        finish(b)
        pl.when(x == b)(lambda: output(b, "stay").start())
        pl.when(right == b)(lambda: output(b, "right").start())
        pl.when(left == b)(lambda: output(b, "left").start())
        pl.when(far == b)(lambda: output(b, "far").start())

    for name in ("right", "left", "far"):
        output(x, name).wait_recv()
    output(x, "stay").wait()
    output(right, "right").wait_send()
    output(left, "left").wait_send()
    output(far, "far").wait_send()
    for copies in (*kv_out.values(), q_out.values(), *hops):
        for copy in copies:
            copy.wait_send()


def body(q, k, v, lengths):
    far_spec = pl.BlockSpec(memory_space=pltpu.HBM)
    dma = pltpu.SemaphoreType.DMA
    q, k, v, lengths = (pltpu.with_memory_space_constraint(a, pltpu.HBM) for a in (q, k, v, lengths))
    return pl.pallas_call(
        kernel,
        out_shape=jax.ShapeDtypeStruct(q.shape, jnp.bfloat16),
        in_specs=[far_spec] * 4,
        out_specs=pl.BlockSpec(memory_space=pl.ANY),
        scratch_shapes=[
            pltpu.SMEM(lengths.shape, jnp.int32),
            pltpu.VMEM((SIDE, ROWS, WIDE), jnp.bfloat16),
            pltpu.VMEM(((REACH + 1) * SIDE, 2, ROWS, HEAD), jnp.bfloat16),
            pltpu.VMEM((SIDE, ROWS, LANES), jnp.int32),
            pltpu.VMEM((SIDE, WIDE, LANES), jnp.float32),
            pltpu.VMEM((SIDE, WIDE, LANES), jnp.float32),
            pltpu.VMEM((SIDE, WIDE, HEAD), jnp.float32),
            pltpu.VMEM((SIDE, ROWS, WIDE), jnp.bfloat16),
            dma((4,)), dma((9,)), dma((9,)), dma((REACH, SIDE)), dma((REACH, SIDE)), dma((3, SIDE)), dma((3, SIDE)),
        ],
        compiler_params=pltpu.CompilerParams(
            collective_id=0, has_side_effects=True, vmem_limit_bytes=32 * 1024 * 1024
        ),
        name="attention",
    )(lengths, q, k, v)


def solution(mesh):
    in_specs = (P(("dp", "ctx"), None), P(("dp", "ctx"), None), P(("dp", "ctx"), None), P("dp"))
    out_specs = P(("dp", "ctx"), None)
    return jax.shard_map(body, mesh=mesh, in_specs=in_specs, out_specs=out_specs, check_vma=False)
```

```python
import math

import jax
import jax.numpy as jnp
from jax import lax
from jax.experimental import pallas as pl
from jax.experimental.pallas import tpu as pltpu
from jax.sharding import PartitionSpec as P

HEAD = 128
ROWS = 128
SIDE = 4
REACH = 3
LANES = 128
WIDE = SIDE * HEAD
MESH = pl.DeviceIdType.MESH
LOWEST = -1e30
RATE = math.log2(math.e) / math.sqrt(HEAD)


def kernel(
    lengths_hbm, q_hbm, k_hbm, v_hbm, out_hbm,
    lengths, q_buf, kv, lo_ref, top, total, acc, o_stage,
    loc_sem, x_send, x_recv, z_send, z_recv, o_send, o_recv,
):
    me = lax.axis_index("ctx")
    count = lax.axis_size("ctx")
    depth = count // SIDE
    z, x = me // SIDE, me % SIDE
    base = z * SIDE
    left, right, far = (x + 3) % SIDE, (x + 1) % SIDE, (x + 2) % SIDE
    above = (me + SIDE) % count
    below = (me + count - SIDE) % count

    def held(row, piece):
        return (REACH - row) * SIDE + piece

    def cols(ref, head, width, start=0, rows=ROWS):
        return ref.at[pl.ds(start, rows), pl.ds(pl.multiple_of(head * width, width), width)]

    local = [
        pltpu.make_async_copy(cols(k_hbm, x, HEAD), kv.at[held(0, x), 0], loc_sem.at[0]),
        pltpu.make_async_copy(cols(v_hbm, x, HEAD), kv.at[held(0, x), 1], loc_sem.at[1]),
        pltpu.make_async_copy(lengths_hbm, lengths, loc_sem.at[2]),
        pltpu.make_async_copy(cols(q_hbm, x, WIDE), q_buf.at[x], loc_sem.at[3]),
    ]

    barrier = pltpu.get_barrier_semaphore()

    def greet(other):
        pl.semaphore_signal(barrier, inc=1, device_id={"ctx": other}, device_id_type=MESH)

    for mate in (left, right, far):
        greet(base + mate)
    pl.when(z > 0)(lambda: greet(below))
    pl.when(z < depth - 1)(lambda: greet(above))

    for copy in local:
        copy.start()
    def clear(b, carry):
        top[b] = jnp.full((WIDE, LANES), LOWEST, jnp.float32)
        total[b] = jnp.zeros((WIDE, LANES), jnp.float32)
        acc[b] = jnp.zeros((WIDE, HEAD), jnp.float32)
        return carry

    lax.fori_loop(0, SIDE, clear, 0)

    def blank(i, carry):
        kv[i] = jnp.zeros((2, ROWS, HEAD), jnp.bfloat16)
        return carry

    lax.fori_loop(0, SIDE * jnp.maximum(REACH - z, 0), blank, 0)
    pl.semaphore_wait(barrier, 3 + jnp.where(z > 0, 1, 0) + jnp.where(z < depth - 1, 1, 0))

    def remote(src, dst, send, recv, to):
        return pltpu.make_async_remote_copy(
            src_ref=src, dst_ref=dst, send_sem=send, recv_sem=recv,
            device_id={"ctx": to}, device_id_type=MESH,
        )

    def x_copy(slot, src, dst, to):
        return remote(src, dst, x_send.at[slot], x_recv.at[slot], base + to)

    def pair(slot, to):
        return [
            x_copy(slot, cols(k_hbm, to, HEAD), kv.at[held(0, x), 0], to),
            x_copy(slot + 1, cols(v_hbm, to, HEAD), kv.at[held(0, x), 1], to),
        ]

    kv_out = {"right": pair(0, right), "left": pair(2, left), "far": pair(4, far)}
    q_out = {
        "right": x_copy(6, cols(q_hbm, right, WIDE), q_buf.at[x], right),
        "left": x_copy(7, cols(q_hbm, left, WIDE), q_buf.at[x], left),
        "far": x_copy(8, cols(q_hbm, far, WIDE), q_buf.at[x], far),
    }
    for copy in kv_out["right"] + kv_out["left"]:
        copy.start()
    for copy in kv_out["far"]:
        copy.start()

    class Hop:
        def __init__(self, row, piece, slot):
            self.row = row
            self.copy = remote(
                kv.at[held(row, piece)], kv.at[held(row + 1, piece)], z_send.at[row, slot], z_recv.at[row, slot], above
            )
            self.sends = (z >= row) & (z < depth - 1)

        def start(self):
            pl.when(self.sends)(self.copy.start)

        def wait_send(self):
            pl.when(self.sends)(self.copy.wait_send)

        def wait_recv(self):
            pl.when(z > self.row)(self.copy.wait_recv)

    order = (
        (x, left, right, far),
        (x, left, jnp.maximum(right, far), jnp.minimum(right, far)),
        (3, 2, 1, 0),
    )
    hops = [[Hop(row, piece, slot) for slot, piece in enumerate(order[row])] for row in range(REACH)]

    local[0].wait()
    local[1].wait()
    hops[0][0].start()
    local[2].wait()

    def starts(b, carry):
        pos = (base + b) * ROWS + lax.broadcasted_iota(jnp.int32, (ROWS, LANES), 0)
        lo = jnp.zeros((ROWS, LANES), jnp.int32)
        bound = jnp.int32(0)
        for i in range(lengths.shape[0]):
            bound = bound + lengths[i]
            lo = jnp.where(pos >= bound, bound, lo)
        lo_ref[b] = lo
        return carry

    lax.fori_loop(0, SIDE, starts, 0)
    for copy in kv_out["right"]:
        copy.wait_recv()
    hops[0][1].start()
    for copy in kv_out["left"]:
        copy.wait_recv()
    hops[0][2].start()
    for copy in kv_out["far"]:
        copy.wait_recv()
    hops[0][3].start()
    for copy in q_out.values():
        copy.start()
    for slot in (0, 1):
        hops[0][slot].wait_recv()
        hops[1][slot].start()
    local[3].wait()

    def attend(b, first, pieces, causal=False):
        n = pieces * ROWS
        heads = [pl.ds(h * ROWS, ROWS) for h in range(SIDE)]
        q = q_buf[b]
        q4 = jnp.concatenate([q[:, h * HEAD:(h + 1) * HEAD] for h in range(SIDE)], axis=0)
        k = kv[pl.ds(first, pieces), 0].reshape(n, HEAD)
        v = kv[pl.ds(first, pieces), 1].reshape(n, HEAD)
        s4 = lax.dot_general(q4, k, (((1,), (1,)), ((), ())), preferred_element_type=jnp.float32)
        start = (base - REACH * SIDE + first) * ROWS
        key_pos = start + lax.broadcasted_iota(jnp.int32, (ROWS, n), 1)
        allowed = key_pos >= jnp.concatenate([lo_ref[b]] * pieces, axis=1)
        if causal:
            allowed = allowed & (key_pos <= (base + b) * ROWS + lax.broadcasted_iota(jnp.int32, (ROWS, n), 0))
        olds = [(top[b, at], total[b, at], acc[b, at]) for at in heads]
        news = []
        for h, (old_top, old_total, old_acc) in enumerate(olds):
            s = jnp.where(allowed, s4[h * ROWS:(h + 1) * ROWS], LOWEST)
            peak = jnp.maximum(old_top, jnp.broadcast_to(jnp.max(s, axis=1, keepdims=True), (ROWS, LANES)))
            fade = jnp.exp2((old_top - peak) * RATE)
            expo = jnp.exp2((s - jnp.concatenate([peak] * pieces, axis=1)) * RATE)
            sums = old_total * fade
            for i in range(pieces):
                sums = sums + expo[:, i * LANES:(i + 1) * LANES]
            mixed = jnp.dot(expo.astype(jnp.bfloat16), v, preferred_element_type=jnp.float32)
            news.append((peak, sums, old_acc * fade + mixed))
        for at, (peak, sums, mixed) in zip(heads, news):
            top[b, at] = peak
            total[b, at] = sums
            acc[b, at] = mixed

    def finish(b):
        for h in range(SIDE):
            at = pl.ds(h * ROWS, ROWS)
            sums = jnp.broadcast_to(jnp.sum(total[b, at], axis=1, keepdims=True), (ROWS, LANES))
            o_stage[b, :, h * HEAD:(h + 1) * HEAD] = (acc[b, at] / sums).astype(jnp.bfloat16)

    def block(step, carry):
        @pl.when(step == 0)
        def _():
            for slot in (2, 3):
                hops[0][slot].wait_recv()
            for slot in (2, 3):
                hops[1][slot].start()

        @pl.when(step == 1)
        def _():
            q_out["right"].wait_recv()

        @pl.when(step == 2)
        def _():
            q_out["left"].wait_recv()

        @pl.when(step == 3)
        def _():
            q_out["far"].wait_recv()
            for slot in (0, 1, 2):
                hops[1][slot].wait_recv()
            hops[2][0].start()

        shift = jnp.where(step == 0, 0, jnp.where(step == 1, 3, step - 1))
        attend((x + shift) % SIDE, 2 * SIDE, 2 * SIDE, True)
        return carry

    lax.fori_loop(0, SIDE, block, 0)
    hops[1][3].wait_recv()
    for slot in (1, 2, 3):
        hops[2][slot].start()

    def o_copy(kind, b, src, dst, to):
        return remote(src, dst, o_send.at[kind, b], o_recv.at[kind, b], base + to)

    def output(b, name):
        near = cols(out_hbm, x, WIDE)
        return {
            "stay": lambda: pltpu.make_async_copy(o_stage.at[b], near, loc_sem.at[0]),
            "right": lambda: o_copy(0, b, o_stage.at[b], near, right),
            "left": lambda: o_copy(1, b, o_stage.at[b], near, left),
            "far": lambda: o_copy(2, b, o_stage.at[b], near, far),
        }[name]()

    @pl.when(z >= 2)
    def _():
        def ahead(b, carry):
            attend(b, SIDE, SIDE)
            return carry

        lax.fori_loop(0, 2, ahead, 0)

    for slot, b in enumerate((3, 2, 1, 0)):
        if b == 0:
            pl.when(z >= REACH)(lambda: attend(b, 1, SIDE - 1))
        hops[2][slot].wait_recv()
        if b == 0:
            pl.when(z >= REACH)(lambda: attend(b, 0, 1))
        elif b == 1:
            pl.when(z >= REACH)(lambda: attend(b, 1, SIDE - 1))
        else:
            pl.when(z >= 2)(lambda: attend(b, b, 2 * SIDE - b))
        finish(b)
        pl.when(x == b)(lambda: output(b, "stay").start())
        pl.when(right == b)(lambda: output(b, "right").start())
        pl.when(left == b)(lambda: output(b, "left").start())
        pl.when(far == b)(lambda: output(b, "far").start())

    for name in ("right", "left", "far"):
        output(x, name).wait_recv()
    output(x, "stay").wait()
    output(right, "right").wait_send()
    output(left, "left").wait_send()
    output(far, "far").wait_send()
    for copies in (*kv_out.values(), q_out.values(), *hops):
        for copy in copies:
            copy.wait_send()


def body(q, k, v, lengths):
    far_spec = pl.BlockSpec(memory_space=pltpu.HBM)
    dma = pltpu.SemaphoreType.DMA
    q, k, v, lengths = (pltpu.with_memory_space_constraint(a, pltpu.HBM) for a in (q, k, v, lengths))
    return pl.pallas_call(
        kernel,
        out_shape=jax.ShapeDtypeStruct(q.shape, jnp.bfloat16),
        in_specs=[far_spec] * 4,
        out_specs=pl.BlockSpec(memory_space=pl.ANY),
        scratch_shapes=[
            pltpu.SMEM(lengths.shape, jnp.int32),
            pltpu.VMEM((SIDE, ROWS, WIDE), jnp.bfloat16),
            pltpu.VMEM(((REACH + 1) * SIDE, 2, ROWS, HEAD), jnp.bfloat16),
            pltpu.VMEM((SIDE, ROWS, LANES), jnp.int32),
            pltpu.VMEM((SIDE, WIDE, LANES), jnp.float32),
            pltpu.VMEM((SIDE, WIDE, LANES), jnp.float32),
            pltpu.VMEM((SIDE, WIDE, HEAD), jnp.float32),
            pltpu.VMEM((SIDE, ROWS, WIDE), jnp.bfloat16),
            dma((4,)), dma((9,)), dma((9,)), dma((REACH, SIDE)), dma((REACH, SIDE)), dma((3, SIDE)), dma((3, SIDE)),
        ],
        compiler_params=pltpu.CompilerParams(
            collective_id=0, has_side_effects=True, vmem_limit_bytes=32 * 1024 * 1024
        ),
        name="attention",
    )(lengths, q, k, v)


def solution(mesh):
    in_specs = (P(("dp", "ctx"), None), P(("dp", "ctx"), None), P(("dp", "ctx"), None), P("dp"))
    out_specs = P(("dp", "ctx"), None)
    return jax.shard_map(body, mesh=mesh, in_specs=in_specs, out_specs=out_specs, check_vma=False)
```

```python
import math

import jax
import jax.numpy as jnp
from jax import lax
from jax.experimental import pallas as pl
from jax.experimental.pallas import tpu as pltpu
from jax.sharding import PartitionSpec as P

HEAD = 128
ROWS = 128
SIDE = 4
REACH = 3
LANES = 128
WIDE = SIDE * HEAD
MESH = pl.DeviceIdType.MESH
LOWEST = -1e30
RATE = math.log2(math.e) / math.sqrt(HEAD)


def kernel(
    lengths_hbm, q_hbm, k_hbm, v_hbm, out_hbm,
    lengths, q_buf, kv, lo_ref, top, total, acc, o_stage,
    loc_sem, x_send, x_recv, z_send, z_recv, o_send, o_recv,
):
    me = lax.axis_index("ctx")
    count = lax.axis_size("ctx")
    depth = count // SIDE
    z, x = me // SIDE, me % SIDE
    base = z * SIDE
    left, right, far = (x + 3) % SIDE, (x + 1) % SIDE, (x + 2) % SIDE
    above = (me + SIDE) % count
    below = (me + count - SIDE) % count

    def held(row, piece):
        return (REACH - row) * SIDE + piece

    def cols(ref, head, width, start=0, rows=ROWS):
        return ref.at[pl.ds(start, rows), pl.ds(pl.multiple_of(head * width, width), width)]

    local = [
        pltpu.make_async_copy(cols(k_hbm, x, HEAD), kv.at[held(0, x), 0], loc_sem.at[0]),
        pltpu.make_async_copy(cols(v_hbm, x, HEAD), kv.at[held(0, x), 1], loc_sem.at[1]),
        pltpu.make_async_copy(lengths_hbm, lengths, loc_sem.at[2]),
        pltpu.make_async_copy(cols(q_hbm, x, WIDE), q_buf.at[x], loc_sem.at[3]),
    ]

    barrier = pltpu.get_barrier_semaphore()

    def greet(other):
        pl.semaphore_signal(barrier, inc=1, device_id={"ctx": other}, device_id_type=MESH)

    for mate in (left, right, far):
        greet(base + mate)
    pl.when(z > 0)(lambda: greet(below))
    pl.when(z < depth - 1)(lambda: greet(above))

    for copy in local:
        copy.start()
    def clear(b, carry):
        top[b] = jnp.full((WIDE, LANES), LOWEST, jnp.float32)
        total[b] = jnp.zeros((WIDE, LANES), jnp.float32)
        acc[b] = jnp.zeros((WIDE, HEAD), jnp.float32)
        return carry

    lax.fori_loop(0, SIDE, clear, 0)

    def blank(i, carry):
        kv[i] = jnp.zeros((2, ROWS, HEAD), jnp.bfloat16)
        return carry

    lax.fori_loop(0, SIDE * jnp.maximum(REACH - z, 0), blank, 0)
    pl.semaphore_wait(barrier, 3 + jnp.where(z > 0, 1, 0) + jnp.where(z < depth - 1, 1, 0))

    def remote(src, dst, send, recv, to):
        return pltpu.make_async_remote_copy(
            src_ref=src, dst_ref=dst, send_sem=send, recv_sem=recv,
            device_id={"ctx": to}, device_id_type=MESH,
        )

    def x_copy(slot, src, dst, to):
        return remote(src, dst, x_send.at[slot], x_recv.at[slot], base + to)

    def pair(slot, to):
        return [
            x_copy(slot, cols(k_hbm, to, HEAD), kv.at[held(0, x), 0], to),
            x_copy(slot + 1, cols(v_hbm, to, HEAD), kv.at[held(0, x), 1], to),
        ]

    kv_out = {"right": pair(0, right), "left": pair(2, left), "far": pair(4, far)}
    q_out = {
        "right": x_copy(6, cols(q_hbm, right, WIDE), q_buf.at[x], right),
        "left": x_copy(7, cols(q_hbm, left, WIDE), q_buf.at[x], left),
        "far": x_copy(8, cols(q_hbm, far, WIDE), q_buf.at[x], far),
    }
    for copy in kv_out["right"] + kv_out["left"]:
        copy.start()
    for copy in kv_out["far"]:
        copy.start()

    class Hop:
        def __init__(self, row, piece, slot):
            self.row = row
            self.copy = remote(
                kv.at[held(row, piece)], kv.at[held(row + 1, piece)], z_send.at[row, slot], z_recv.at[row, slot], above
            )
            self.sends = (z >= row) & (z < depth - 1)

        def start(self):
            pl.when(self.sends)(self.copy.start)

        def wait_send(self):
            pl.when(self.sends)(self.copy.wait_send)

        def wait_recv(self):
            pl.when(z > self.row)(self.copy.wait_recv)

    order = (
        (x, left, right, far),
        (x, left, jnp.maximum(right, far), jnp.minimum(right, far)),
        (3, 2, 1, 0),
    )
    hops = [[Hop(row, piece, slot) for slot, piece in enumerate(order[row])] for row in range(REACH)]

    local[0].wait()
    local[1].wait()
    hops[0][0].start()
    local[2].wait()

    def starts(b, carry):
        pos = (base + b) * ROWS + lax.broadcasted_iota(jnp.int32, (ROWS, LANES), 0)
        lo = jnp.zeros((ROWS, LANES), jnp.int32)
        bound = jnp.int32(0)
        for i in range(lengths.shape[0]):
            bound = bound + lengths[i]
            lo = jnp.where(pos >= bound, bound, lo)
        lo_ref[b] = lo
        return carry

    lax.fori_loop(0, SIDE, starts, 0)
    for copy in kv_out["right"]:
        copy.wait_recv()
    hops[0][1].start()
    for copy in kv_out["left"]:
        copy.wait_recv()
    hops[0][2].start()
    for copy in kv_out["far"]:
        copy.wait_recv()
    hops[0][3].start()
    for copy in q_out.values():
        copy.start()
    for slot in (0, 1):
        hops[0][slot].wait_recv()
        hops[1][slot].start()
    local[3].wait()

    def attend(b, first, pieces, causal=False):
        n = pieces * ROWS
        heads = [pl.ds(h * ROWS, ROWS) for h in range(SIDE)]
        q = q_buf[b]
        q4 = jnp.concatenate([q[:, h * HEAD:(h + 1) * HEAD] for h in range(SIDE)], axis=0)
        k = kv[pl.ds(first, pieces), 0].reshape(n, HEAD)
        v = kv[pl.ds(first, pieces), 1].reshape(n, HEAD)
        s4 = lax.dot_general(q4, k, (((1,), (1,)), ((), ())), preferred_element_type=jnp.float32)
        start = (base - REACH * SIDE + first) * ROWS
        key_pos = start + lax.broadcasted_iota(jnp.int32, (ROWS, n), 1)
        allowed = key_pos >= jnp.concatenate([lo_ref[b]] * pieces, axis=1)
        if causal:
            early = n - SIDE * ROWS
            q_pos = (base + b) * ROWS + lax.broadcasted_iota(jnp.int32, (ROWS, SIDE * ROWS), 0)
            allowed = jnp.concatenate([allowed[:, :early], allowed[:, early:] & (key_pos[:, early:] <= q_pos)], axis=1)
        olds = [(top[b, at], total[b, at], acc[b, at]) for at in heads]
        news = []
        for h, (old_top, old_total, old_acc) in enumerate(olds):
            s = jnp.where(allowed, s4[h * ROWS:(h + 1) * ROWS], LOWEST)
            peak = jnp.maximum(old_top, jnp.broadcast_to(jnp.max(s, axis=1, keepdims=True), (ROWS, LANES)))
            fade = jnp.exp2((old_top - peak) * RATE)
            expo = jnp.exp2((s - jnp.concatenate([peak] * pieces, axis=1)) * RATE)
            sums = old_total * fade
            for i in range(pieces):
                sums = sums + expo[:, i * LANES:(i + 1) * LANES]
            mixed = jnp.dot(expo.astype(jnp.bfloat16), v, preferred_element_type=jnp.float32)
            news.append((peak, sums, old_acc * fade + mixed))
        for at, (peak, sums, mixed) in zip(heads, news):
            top[b, at] = peak
            total[b, at] = sums
            acc[b, at] = mixed

    def finish(b):
        for h in range(SIDE):
            at = pl.ds(h * ROWS, ROWS)
            sums = jnp.broadcast_to(jnp.sum(total[b, at], axis=1, keepdims=True), (ROWS, LANES))
            o_stage[b, :, h * HEAD:(h + 1) * HEAD] = (acc[b, at] / sums).astype(jnp.bfloat16)

    def block(step, carry):
        @pl.when(step == 0)
        def _():
            for slot in (2, 3):
                hops[0][slot].wait_recv()
            for slot in (2, 3):
                hops[1][slot].start()

        @pl.when(step == 1)
        def _():
            q_out["right"].wait_recv()

        @pl.when(step == 2)
        def _():
            q_out["left"].wait_recv()

        @pl.when(step == 3)
        def _():
            q_out["far"].wait_recv()
            for slot in (0, 1, 2):
                hops[1][slot].wait_recv()
            hops[2][0].start()

        shift = jnp.where(step == 0, 0, jnp.where(step == 1, 3, step - 1))
        attend((x + shift) % SIDE, 2 * SIDE, 2 * SIDE, True)
        return carry

    lax.fori_loop(0, SIDE, block, 0)
    hops[1][3].wait_recv()
    for slot in (1, 2, 3):
        hops[2][slot].start()

    def o_copy(kind, b, src, dst, to):
        return remote(src, dst, o_send.at[kind, b], o_recv.at[kind, b], base + to)

    def output(b, name):
        near = cols(out_hbm, x, WIDE)
        return {
            "stay": lambda: pltpu.make_async_copy(o_stage.at[b], near, loc_sem.at[0]),
            "right": lambda: o_copy(0, b, o_stage.at[b], near, right),
            "left": lambda: o_copy(1, b, o_stage.at[b], near, left),
            "far": lambda: o_copy(2, b, o_stage.at[b], near, far),
        }[name]()

    @pl.when(z >= 2)
    def _():
        def ahead(b, carry):
            attend(b, SIDE, SIDE)
            return carry

        lax.fori_loop(0, 2, ahead, 0)

    for slot, b in enumerate((3, 2, 1, 0)):
        if b == 0:
            pl.when(z >= REACH)(lambda: attend(b, 1, SIDE - 1))
        hops[2][slot].wait_recv()
        if b == 0:
            pl.when(z >= REACH)(lambda: attend(b, 0, 1))
        elif b == 1:
            pl.when(z >= REACH)(lambda: attend(b, 1, SIDE - 1))
        else:
            pl.when(z >= 2)(lambda: attend(b, b, 2 * SIDE - b))
        finish(b)
        pl.when(x == b)(lambda: output(b, "stay").start())
        pl.when(right == b)(lambda: output(b, "right").start())
        pl.when(left == b)(lambda: output(b, "left").start())
        pl.when(far == b)(lambda: output(b, "far").start())

    for name in ("right", "left", "far"):
        output(x, name).wait_recv()
    output(x, "stay").wait()
    output(right, "right").wait_send()
    output(left, "left").wait_send()
    output(far, "far").wait_send()
    for copies in (*kv_out.values(), q_out.values(), *hops):
        for copy in copies:
            copy.wait_send()


def body(q, k, v, lengths):
    far_spec = pl.BlockSpec(memory_space=pltpu.HBM)
    dma = pltpu.SemaphoreType.DMA
    q, k, v, lengths = (pltpu.with_memory_space_constraint(a, pltpu.HBM) for a in (q, k, v, lengths))
    return pl.pallas_call(
        kernel,
        out_shape=jax.ShapeDtypeStruct(q.shape, jnp.bfloat16),
        in_specs=[far_spec] * 4,
        out_specs=pl.BlockSpec(memory_space=pl.ANY),
        scratch_shapes=[
            pltpu.SMEM(lengths.shape, jnp.int32),
            pltpu.VMEM((SIDE, ROWS, WIDE), jnp.bfloat16),
            pltpu.VMEM(((REACH + 1) * SIDE, 2, ROWS, HEAD), jnp.bfloat16),
            pltpu.VMEM((SIDE, ROWS, LANES), jnp.int32),
            pltpu.VMEM((SIDE, WIDE, LANES), jnp.float32),
            pltpu.VMEM((SIDE, WIDE, LANES), jnp.float32),
            pltpu.VMEM((SIDE, WIDE, HEAD), jnp.float32),
            pltpu.VMEM((SIDE, ROWS, WIDE), jnp.bfloat16),
            dma((4,)), dma((9,)), dma((9,)), dma((REACH, SIDE)), dma((REACH, SIDE)), dma((3, SIDE)), dma((3, SIDE)),
        ],
        compiler_params=pltpu.CompilerParams(
            collective_id=0, has_side_effects=True, vmem_limit_bytes=32 * 1024 * 1024
        ),
        name="attention",
    )(lengths, q, k, v)


def solution(mesh):
    in_specs = (P(("dp", "ctx"), None), P(("dp", "ctx"), None), P(("dp", "ctx"), None), P("dp"))
    out_specs = P(("dp", "ctx"), None)
    return jax.shard_map(body, mesh=mesh, in_specs=in_specs, out_specs=out_specs, check_vma=False)
```
